32 devices in a mesh: group: 2 (over y), pool: 4 (over x, core), sub: 4 (over z).
Axes of the slice: x: 2, y: 2, z: 4, core: 2. Of those that a mesh axis runs over, the one named last changes fastest.
Arguments:
- hidden_in: bfloat16 [3, 128, 4096], P(None, ('group', 'pool', 'sub')), parts along dimension 1, may hold values from -6 to 6
- norm_gain: bfloat16 [4096], replicated, may hold values from 0.25 to 1.75
- expert_ids: int32 [3, 128, 8], P(None, ('group', 'pool', 'sub')), parts along dimension 1, may hold values from 0 to 31, all different within a row; in each aligned block of 4 rows (0 to 3, 4 to 7, ..., all dimensions but the last counted through in order) at most 2 rows name the same one
- gate_weights: bfloat16 [3, 128, 8], P(None, ('group', 'pool', 'sub')), parts along dimension 1, may hold values from 0.049804688 to 1
- w_gate: bfloat16 [32, 4096, 1536], P('pool', None, 'sub'), may hold values from -0.09375 to 0.09375
- w_up: bfloat16 [32, 4096, 1536], P('pool', None, 'sub'), may hold values from -0.09375 to 0.09375
- w_down: bfloat16 [32, 1536, 4096], P('pool', 'sub'), may hold values from -0.15625 to 0.15625
Outputs:
- layer_out: bfloat16 [3, 128, 4096], P(None, ('group', 'pool', 'sub')), parts along dimension 1
The draws below stay inside these ranges and needn't reach their ends.
There are 2 independent parts, one for each index of `group`. The reference program is written for one: setup_inputs(seed, part) draws one part's arguments, and reference() takes and returns one part's arrays. A program takes and returns all parts, laid end to end along the dimension named above; an argument that names none is the same for every part. Nothing has to cross between parts.
Inputs may be any that keep to these rules, and one draw needn't show every extreme that they name: `expert_ids`: the 8 entries of a row differ. In each aligned block of 4 rows of one micro-batch (the rows of one device) no expert is named by more than 2 rows, a bound that some block reaches.
All inputs are finite; a program needn't handle non-finite values.
Results may differ from the reference program's by a relative error of at most 0.0095.
Values may be sent and summed in bfloat16 or wider, within the bound.
A program may use at most 192 MiB of HBM per device.

```python
import math
import jax
import jax.numpy as jnp
import numpy as np
from jax import lax

D = 4096
HIDDEN_SIZE = 1536
TOP = 8
EXPERTS = 32
MICRO = 3
ROWS_DEV = 4
CAP = 2
ROWS = 64
N_POOL = 4
N_SUB = 4


def levels(own_key, extent, shards, smallest, largest):
    level, own = 1.0, jax.random.fold_in(own_key, 6)
    for axis_at, parts in shards:
        heights = jnp.exp(jax.random.uniform(jax.random.fold_in(own, axis_at), (parts,), jnp.float32, smallest / len(shards), largest / len(shards)))
        level = level * jnp.repeat(heights, extent[axis_at] // parts).reshape([-1 if axis == axis_at else 1 for axis in range(len(extent))])
    return level


def assign_block(rng, own, number, rows, amount, top, limit, skew):
    ranking = jax.random.permutation(rng, amount)
    packed, usual = load_shares(amount, rows * top, limit, skew, True), load_shares(amount, rows * top, limit, skew, False)
    places = jnp.arange(amount)

    def named(tallies, turn):
        used = int((tallies > 0).sum())
        fixed = max(1, used // 4)
        passed = fixed + (places - fixed + turn * (used - fixed)) % max(1, amount - fixed)
        return jnp.zeros((amount,), jnp.int32).at[ranking[jnp.where(places < fixed, places, passed)]].set(jnp.asarray(tallies, jnp.int32))

    tallies = jnp.where(number % 4 == 0, named(packed, number // 4), named(usual, number - number // 4 - 1))
    mixed = jax.random.permutation(jax.random.fold_in(own, 3), amount)
    giver, taker = mixed[0:amount // 2 * 2:2], mixed[1:amount // 2 * 2:2]
    room = jnp.minimum(tallies[giver] - 1, limit - tallies[taker]) // 2
    room = jnp.where((giver == ranking[0]) | (taker == ranking[0]) | (tallies[taker] == 0), 0, jnp.maximum(room, 0))
    passed = jax.random.randint(jax.random.fold_in(own, 4), (amount // 2,), 0, 1 << 20) % (room + 1)
    tallies = tallies.at[giver].add(-passed).at[taker].add(passed)
    members = jnp.searchsorted(jnp.cumsum(tallies), jnp.arange(rows * top), side="right").astype(jnp.int32)
    grid = members.reshape(top, rows).T
    grid = grid[jax.random.permutation(jax.random.fold_in(own, 1), rows)]
    turn = jax.random.randint(jax.random.fold_in(own, 2), (rows, 1), 0, top)
    return jnp.take_along_axis(grid, (jnp.arange(top)[None, :] + turn) % top, axis=1)


def load_shares(number_of, total, most, lean, full):
    loads = [(1 << 20) // math.isqrt(rank ** lean) + 1 for rank in range(1, number_of + 1)]
    largest = most if full else min(most, max(-(-total // number_of), total * loads[0] // sum(loads)))
    least = 1 if total - largest >= number_of - 1 else 0
    holding, surplus = [largest] + [least] * (number_of - 1), total - largest - least * (number_of - 1)
    while surplus > 0:
        free = [i for i in range(1, number_of) if holding[i] < largest] or [i for i in range(1, number_of) if holding[i] < most]
        mass, left = sum([loads[i] for i in free]), surplus
        for i in free:
            more = min(most - holding[i], max(1, left * loads[i] // mass), surplus)
            holding[i] = holding[i] + more
            surplus = surplus - more
    return np.array(holding)


def bell_draw(stream_key, shape, deviation, bound, cuts=(), kind=jnp.bfloat16):
    gain = levels(stream_key, shape, cuts, -0.22, 0.18) if cuts else 1.0
    drawn = jax.random.normal(stream_key, shape, jnp.float32) * deviation * gain
    return jnp.minimum(jnp.maximum(drawn, -bound), bound).astype(kind)


def setup_inputs(seed: int = 0, part: int = 0) -> dict:
    key_of = jax.random.split(jax.random.key(seed), 8)
    own_keys = jax.random.split(jax.random.fold_in(key_of[7], part), 8)
    hidden_in = bell_draw(own_keys[0], (MICRO, ROWS, D), 1.0, 6.0, ((1, 16),))
    norm_gain = jnp.clip(1.0 + 0.15 * jax.random.normal(key_of[1], (D,), jnp.float32), 0.25, 1.75).astype(jnp.bfloat16)
    expert_ids_keys = jax.random.split(jax.random.fold_in(own_keys[2], 1), MICRO * ROWS // ROWS_DEV)
    expert_ids_turns = jax.random.permutation(jax.random.fold_in(own_keys[2], 3), MICRO * ROWS // ROWS_DEV)
    expert_ids = jax.vmap(lambda own, number: assign_block(jax.random.fold_in(own_keys[2], 2), own, number, ROWS_DEV, EXPERTS, TOP, CAP, 2))(expert_ids_keys, expert_ids_turns).reshape((MICRO, ROWS, TOP))
    gate_weights = jnp.clip(jnp.exp(math.log(1.0) - 2.9996462 * jax.random.uniform(own_keys[3], (MICRO, ROWS, TOP), jnp.float32) ** levels(own_keys[3], (MICRO, ROWS, TOP), ((1, 16),), -0.2, 0.2)), 0.049804688, 1.0).astype(jnp.bfloat16)
    w_gate = bell_draw(key_of[4], (EXPERTS, D, HIDDEN_SIZE), D ** -0.5, 0.09375, ((0, 4), (2, 4)))
    w_up = bell_draw(key_of[5], (EXPERTS, D, HIDDEN_SIZE), D ** -0.5, 0.09375, ((0, 4), (2, 4)))
    w_down = bell_draw(key_of[6], (EXPERTS, HIDDEN_SIZE, D), HIDDEN_SIZE ** -0.5, 0.15625, ((0, 4), (1, 4)))
    return dict(hidden_in=hidden_in, norm_gain=norm_gain, expert_ids=expert_ids, gate_weights=gate_weights, w_gate=w_gate, w_up=w_up, w_down=w_down)


def reference(hidden_in, norm_gain, expert_ids, gate_weights, w_gate, w_up, w_down):
    devices_part = N_POOL * N_SUB
    values = hidden_in.astype(jnp.float32)
    scale = lax.rsqrt(lax.optimization_barrier(jnp.mean(values * values, axis=-1, keepdims=True)) + 1e-06)
    normed = (values * scale * norm_gain.astype(jnp.float32)).astype(jnp.bfloat16).reshape(MICRO * ROWS, D)
    blocks = expert_ids.reshape(MICRO * devices_part, ROWS_DEV * TOP)
    onehot = (blocks[..., None] == jnp.arange(EXPERTS, dtype=jnp.int32)).astype(jnp.int32)
    earlier = jnp.cumsum(onehot, axis=1) - onehot
    position = lax.optimization_barrier(jnp.sum(earlier * onehot, axis=-1)).astype(jnp.int32)
    block_number = jnp.arange(MICRO * devices_part, dtype=jnp.int32)[:, None]
    column = block_number * CAP + position
    token_row = block_number * ROWS_DEV + (jnp.arange(ROWS_DEV * TOP, dtype=jnp.int32) // TOP)[None, :]
    slot_count = MICRO * devices_part * CAP
    table = jnp.full((EXPERTS, slot_count), -1, jnp.int32).at[blocks, column].set(token_row)
    gate_table = jnp.zeros((EXPERTS, slot_count), jnp.float32).at[blocks, column].set(gate_weights.reshape(blocks.shape).astype(jnp.float32))
    block_width = HIDDEN_SIZE // N_SUB

    def one_expert(operands):
        table_row, gate_row, gate_mat, up_mat, down_mat = operands
        valid = table_row >= 0
        picked = jnp.where(valid[:, None], normed[jnp.maximum(table_row, 0)], jnp.zeros((), jnp.bfloat16))
        gate_act = jnp.dot(picked, gate_mat, preferred_element_type=jnp.float32)
        up_act = jnp.dot(picked, up_mat, preferred_element_type=jnp.float32)
        activ = (jax.nn.silu(gate_act) * up_act).astype(jnp.bfloat16)
        pieces = jnp.einsum('csh,shd->scd', activ.reshape(slot_count, N_SUB, block_width).astype(jnp.float32), down_mat.reshape(N_SUB, block_width, D).astype(jnp.float32))
        rounded = lax.optimization_barrier(pieces.astype(jnp.bfloat16)).astype(jnp.float32)
        summed = lax.optimization_barrier(jnp.sum(rounded, axis=0))
        return (summed * gate_row[:, None]).astype(jnp.bfloat16)
    weighted = lax.map(one_expert, (table, gate_table, w_gate, w_up, w_down))
    flat_valid = (table >= 0).reshape(-1)
    contrib = jnp.where(flat_valid[:, None], weighted.reshape(-1, D).astype(jnp.float32), jnp.zeros((), jnp.float32))
    accumulated = jnp.zeros((MICRO * ROWS, D), jnp.float32).at[jnp.maximum(table, 0).reshape(-1)].add(contrib)
    return (values.reshape(MICRO * ROWS, D) + accumulated).astype(jnp.bfloat16).reshape(MICRO, ROWS, D)
```

```python
import jax
import jax.numpy as jnp
from jax import lax
from jax.sharding import PartitionSpec as P


def rms_normed(hidden, norm_gain):
    values = hidden.astype(jnp.float32)
    scale = lax.rsqrt(jnp.mean(values * values, axis=-1, keepdims=True) + 1e-06)
    return (values * scale * norm_gain.astype(jnp.float32)).astype(jnp.bfloat16)


def dense_body(hidden_in, norm_gain, expert_ids, gate_weights, w_gate, w_up, w_down):
    batches, row_count, width = hidden_in.shape
    per_pool, _, hid = w_gate.shape
    pools = lax.axis_size("pool")
    own = batches * row_count
    normed = rms_normed(hidden_in, norm_gain).reshape(own, width)
    experts = jnp.arange(pools * per_pool, dtype=jnp.int32)
    gates = jnp.sum(
        jnp.where(expert_ids[..., None] == experts, gate_weights[..., None].astype(jnp.float32), 0.0), axis=2
    ).astype(jnp.bfloat16).reshape(own, pools * per_pool)
    rows = lax.all_gather(normed, ("pool", "sub"), axis=0, tiled=True)
    gates = lax.all_gather(gates, ("pool", "sub"), axis=0, tiled=True)
    gates = lax.dynamic_slice_in_dim(gates, lax.axis_index("pool") * per_pool, per_pool, axis=1)
    acts = []
    for e in range(per_pool):
        gate_act = jnp.dot(rows, w_gate[e], preferred_element_type=jnp.float32)
        up_act = jnp.dot(rows, w_up[e], preferred_element_type=jnp.float32)
        weight = gates[:, e : e + 1].astype(jnp.float32)
        acts.append((jax.nn.silu(gate_act) * up_act * weight).astype(jnp.bfloat16))
    act = jnp.concatenate(acts, axis=1)
    partial = jnp.dot(act, w_down.reshape(per_pool * hid, width), preferred_element_type=jnp.float32)
    summed = lax.psum_scatter(partial.astype(jnp.bfloat16), ("pool", "sub"), scatter_dimension=0, tiled=True)
    result = hidden_in.reshape(own, width).astype(jnp.float32) + summed.astype(jnp.float32)
    return result.astype(jnp.bfloat16).reshape(batches, row_count, width)


def solution(mesh):
    in_specs = (
        P(None, ("group", "pool", "sub"), None),
        P(),
        P(None, ("group", "pool", "sub"), None),
        P(None, ("group", "pool", "sub"), None),
        P("pool", None, "sub"),
        P("pool", None, "sub"),
        P("pool", "sub", None),
    )
    out_specs = P(None, ("group", "pool", "sub"), None)
    return jax.shard_map(dense_body, mesh=mesh, in_specs=in_specs, out_specs=out_specs, check_vma=False)
```

```python
import functools

import jax
import jax.numpy as jnp
from jax import lax
from jax.experimental import pallas as pl
from jax.experimental.pallas import tpu as pltpu
from jax.sharding import PartitionSpec as P


def rms_normed(hidden, norm_gain):
    values = hidden.astype(jnp.float32)
    scale = lax.rsqrt(jnp.mean(values * values, axis=-1, keepdims=True) + 1e-06)
    return (values * scale * norm_gain.astype(jnp.float32)).astype(jnp.bfloat16)


def dense_body(hidden_in, norm_gain, expert_ids, gate_weights, w_gate, w_up, w_down):
    batches, row_count, width = hidden_in.shape
    per_pool, _, hid = w_gate.shape
    pools = lax.axis_size("pool")
    own = batches * row_count
    normed = rms_normed(hidden_in, norm_gain).reshape(own, width)
    experts = jnp.arange(pools * per_pool, dtype=jnp.int32)
    gates = jnp.sum(
        jnp.where(expert_ids[..., None] == experts, gate_weights[..., None].astype(jnp.float32), 0.0), axis=2
    ).astype(jnp.bfloat16).reshape(own, pools * per_pool)
    rows = lax.all_gather(normed, ("pool", "sub"), axis=0, tiled=True)
    gates = lax.all_gather(gates, ("pool", "sub"), axis=0, tiled=True)
    gates = lax.dynamic_slice_in_dim(gates, lax.axis_index("pool") * per_pool, per_pool, axis=1)
    acts = []
    for e in range(per_pool):
        gate_act = jnp.dot(rows, w_gate[e], preferred_element_type=jnp.float32)
        up_act = jnp.dot(rows, w_up[e], preferred_element_type=jnp.float32)
        weight = gates[:, e : e + 1].astype(jnp.float32)
        acts.append((jax.nn.silu(gate_act) * up_act * weight).astype(jnp.bfloat16))
    act = jnp.concatenate(acts, axis=1)
    partial = jnp.dot(act, w_down.reshape(per_pool * hid, width), preferred_element_type=jnp.float32)
    summed = lax.psum_scatter(partial.astype(jnp.bfloat16), ("pool", "sub"), scatter_dimension=0, tiled=True)
    result = hidden_in.reshape(own, width).astype(jnp.float32) + summed.astype(jnp.float32)
    return result.astype(jnp.bfloat16).reshape(batches, row_count, width)


MESH = pl.DeviceIdType.MESH
F32 = jnp.float32
BF16 = jnp.bfloat16
PAD = 16
GW = 128
KC = 4
NC = 8
SLOTS = 12


def expert_kernel(
    subs, hidden, gain, ids, gws, w_gate, w_up, w_down, out,
    xg, acc, act, y, crecv, xsend, xrecv, zsend, zrecv, gu, wd, rowf, sumf,
    gu_sem, wd_sem, az_s, az_r, ax_s, ax_r, ac_s, ac_r,
    rc_s, rc_r, rx_s, rx_r, rz_s, rz_r,
):
    batches, rows, width = hidden.shape
    per_pool, _, hid = w_gate.shape
    kw, nw = width // KC, width // NC
    group, pool, sub = lax.axis_index("group"), lax.axis_index("pool"), lax.axis_index("sub")
    core, side = pool % 2, pool // 2
    quad = subs * PAD
    half = 2 * quad
    xrow = core * half + side * quad
    own = pl.multiple_of(xrow + sub * PAD, PAD)
    peer_core = (group, side * 2 + 1 - core, sub)
    peer_side = (group, (1 - side) * 2 + core, sub)
    peer_sub = [(group, pool, (sub + d) % subs) for d in range(1, subs)]
    steps = KC * per_pool

    def gu_copies(step):
        slot, e = step % SLOTS, step % per_pool
        krow = pl.multiple_of(step // per_pool * kw, kw)
        return (
            pltpu.make_async_copy(w_gate.at[e, pl.ds(krow, kw), :], gu.at[slot, :, pl.ds(0, hid)], gu_sem.at[slot, 0]),
            pltpu.make_async_copy(w_up.at[e, pl.ds(krow, kw), :], gu.at[slot, :, pl.ds(hid, hid)], gu_sem.at[slot, 1]),
        )

    def wd_copy(n):
        return pltpu.make_async_copy(
            w_down.at[:, :, pl.ds(pl.multiple_of(n * nw, nw), nw)], wd.at[n], wd_sem.at[n]
        )

    def first(step, carry):
        for copy in gu_copies(step):
            copy.start()
        return carry

    lax.fori_loop(0, SLOTS, first, 0)

    barrier = pltpu.get_barrier_semaphore()
    for peer in [peer_core, peer_side] + peer_sub:
        pl.semaphore_signal(barrier, inc=1, device_id=peer, device_id_type=MESH)

    rowf[...] = jnp.zeros_like(rowf)
    lane = lax.broadcasted_iota(jnp.int32, (rows, GW), 1)
    gain_row = gain[...].astype(F32)
    for m in range(batches):
        values = hidden[m].astype(F32)
        scale = lax.rsqrt(jnp.mean(values * values, axis=-1, keepdims=True) + 1e-06)
        rowf[rows * m : rows * (m + 1), GW:] = values * scale * gain_row
        names, weights = ids[m], gws[m].astype(F32)
        table = jnp.zeros((rows, GW), F32)
        for k in range(names.shape[1]):
            table = table + jnp.where(names[:, k : k + 1] == lane, weights[:, k : k + 1], 0.0)
        rowf[rows * m : rows * (m + 1), :GW] = table
    xg[pl.ds(own, PAD), :] = rowf[...].astype(BF16)

    pl.semaphore_wait(barrier, subs + 1)

    def cols(c):
        return pl.ds(0, GW + kw) if c == 0 else pl.ds(GW + c * kw, kw)

    def az(c, d):
        ref = xg.at[pl.ds(own, PAD), cols(c)]
        return pltpu.make_async_remote_copy(
            ref, ref, az_s.at[c, d], az_r.at[c, d], device_id=peer_sub[d], device_id_type=MESH
        )

    def az_wait(c):
        for d in range(subs - 1):
            az(c, d).wait_recv()

    def ax(c):
        ref = xg.at[pl.ds(pl.multiple_of(xrow, PAD), quad), cols(c)]
        return pltpu.make_async_remote_copy(
            ref, ref, ax_s.at[c], ax_r.at[c], device_id=peer_side, device_id_type=MESH
        )

    def ac(c):
        ref = xg.at[pl.ds(pl.multiple_of(core * half, PAD), half), cols(c)]
        return pltpu.make_async_remote_copy(
            ref, ref, ac_s.at[c], ac_r.at[c], device_id=peer_core, device_id_type=MESH
        )

    def relay_x(c):
        az_wait(c)
        ax(c).start()

    def relay_c(c):
        ax(c).wait_recv()
        ac(c).start()

    for c in range(KC):
        for d in range(subs - 1):
            az(c, d).start()
    acc[...] = jnp.zeros_like(acc)
    relay_x(0)
    relay_x(1)
    relay_c(0)

    def gu_step(c, step, carry):
        slot, e = step % SLOTS, step % per_pool
        for copy in gu_copies(step):
            copy.wait()
        total = acc[e] + jnp.dot(
            xg[:, GW + c * kw : GW + (c + 1) * kw], gu[slot], preferred_element_type=F32
        )
        if c < KC - 1:
            acc[e] = total
        else:
            g, u = total[:, :hid], total[:, hid:]
            lanes = lax.broadcasted_iota(jnp.int32, (2 * half, GW), 1)
            weight = jnp.sum(
                jnp.where(lanes == pool * per_pool + e, xg[:, :GW].astype(F32), 0.0), axis=1, keepdims=True
            )
            act[:, pl.ds(pl.multiple_of(e * hid, hid), hid)] = (
                g / (1.0 + jnp.exp(-g)) * u * weight
            ).astype(BF16)

        @pl.when(step + SLOTS < steps)
        def _():
            for copy in gu_copies(step + SLOTS):
                copy.start()

        extra = step + SLOTS - steps

        @pl.when((extra >= 0) & (extra < NC))
        def _():
            wd_copy(extra).start()

        return carry

    cut = per_pool // 2
    for c in range(KC):
        ac(c).wait_recv()
        base = c * per_pool
        lax.fori_loop(base, base + cut, functools.partial(gu_step, c), 0)
        if c + 2 < KC:
            relay_x(c + 2)
        if c + 1 < KC:
            relay_c(c + 1)
        lax.fori_loop(base + cut, base + per_pool, functools.partial(gu_step, c), 0)

    def ncols(n):
        return pl.ds(pl.multiple_of(n * nw, nw), nw)

    def rc(n):
        return pltpu.make_async_remote_copy(
            y.at[pl.ds(pl.multiple_of((1 - core) * half, PAD), half), ncols(n)], crecv.at[:, ncols(n)],
            rc_s.at[n], rc_r.at[n], device_id=peer_core, device_id_type=MESH,
        )

    def rx(n):
        return pltpu.make_async_remote_copy(
            xsend.at[:, ncols(n)], xrecv.at[:, ncols(n)],
            rx_s.at[n], rx_r.at[n], device_id=peer_side, device_id_type=MESH,
        )

    def rz(n, d):
        row = pl.multiple_of((sub + d + 1) % subs * PAD, PAD)
        return pltpu.make_async_remote_copy(
            zsend.at[pl.ds(row, PAD), ncols(n)], zrecv.at[d, :, ncols(n)],
            rz_s.at[n, d], rz_r.at[n, d], device_id=peer_sub[d], device_id_type=MESH,
        )

    def down_step(n, carry):
        @pl.when(n < NC)
        def _():
            wd_copy(n).wait()
            y[:, ncols(n)] = jnp.dot(
                act[...], wd[n].reshape(per_pool * hid, nw), preferred_element_type=F32
            ).astype(BF16)
            rc(n).start()

        @pl.when((n >= 1) & (n < NC + 1))
        def _():
            m = n - 1
            rc(m).wait_recv()
            far = pl.multiple_of((1 - side) * quad, PAD)
            xsend[:, ncols(m)] = (
                y[pl.ds(pl.multiple_of(core * half + (1 - side) * quad, PAD), quad), ncols(m)].astype(F32)
                + crecv[pl.ds(far, quad), ncols(m)].astype(F32)
            ).astype(BF16)
            rx(m).start()

        @pl.when((n >= 2) & (n < NC + 2))
        def _():
            m = n - 2
            rx(m).wait_recv()
            near = pl.multiple_of(side * quad, PAD)
            zsend[:, ncols(m)] = (
                y[pl.ds(pl.multiple_of(xrow, PAD), quad), ncols(m)].astype(F32)
                + crecv[pl.ds(near, quad), ncols(m)].astype(F32)
                + xrecv[:, ncols(m)].astype(F32)
            ).astype(BF16)
            for d in range(subs - 1):
                rz(m, d).start()

        @pl.when(n >= 3)
        def _():
            m = n - 3
            total = zsend[pl.ds(pl.multiple_of(sub * PAD, PAD), PAD), ncols(m)].astype(F32)
            for d in range(subs - 1):
                rz(m, d).wait_recv()
                total = total + zrecv[d, :, ncols(m)].astype(F32)
            sumf[...] = total
            for b in range(batches):
                out[b, :, ncols(m)] = (
                    hidden[b, :, ncols(m)].astype(F32) + sumf[rows * b : rows * (b + 1), :]
                ).astype(BF16)

        return carry

    lax.fori_loop(0, NC + 3, down_step, 0)

    for c in range(KC):
        for d in range(subs - 1):
            az(c, d).wait_send()
        ax(c).wait_send()
        ac(c).wait_send()

    def sent(n, carry):
        rc(n).wait_send()
        rx(n).wait_send()
        for d in range(subs - 1):
            rz(n, d).wait_send()
        return carry

    lax.fori_loop(0, NC, sent, 0)


def kernel_body(hidden_in, norm_gain, expert_ids, gate_weights, w_gate, w_up, w_down):
    batches, rows, width = hidden_in.shape
    per_pool, _, hid = w_gate.shape
    subs = lax.axis_size("sub")
    total = 4 * subs * PAD
    vmem = pl.BlockSpec(memory_space=pltpu.VMEM)
    hbm = pl.BlockSpec(memory_space=pl.ANY)
    dma = pltpu.SemaphoreType.DMA
    others = subs - 1
    return pl.pallas_call(
        functools.partial(expert_kernel, subs),
        out_shape=jax.ShapeDtypeStruct(hidden_in.shape, BF16),
        in_specs=[vmem] * 4 + [hbm] * 3,
        out_specs=vmem,
        scratch_shapes=[
            pltpu.VMEM((total, GW + width), BF16),
            pltpu.VMEM((per_pool, total, 2 * hid), F32),
            pltpu.VMEM((total, per_pool * hid), BF16),
            pltpu.VMEM((total, width), BF16),
            pltpu.VMEM((total // 2, width), BF16),
            pltpu.VMEM((total // 4, width), BF16),
            pltpu.VMEM((total // 4, width), BF16),
            pltpu.VMEM((total // 4, width), BF16),
            pltpu.VMEM((others, PAD, width), BF16),
            pltpu.VMEM((SLOTS, width // KC, 2 * hid), BF16),
            pltpu.VMEM((NC, per_pool, hid, width // NC), BF16),
            pltpu.VMEM((PAD, GW + width), F32),
            pltpu.VMEM((PAD, width // NC), F32),
            dma((SLOTS, 2)),
            dma((NC,)),
            dma((KC, others)),
            dma((KC, others)),
            dma((KC,)),
            dma((KC,)),
            dma((KC,)),
            dma((KC,)),
            dma((NC,)),
            dma((NC,)),
            dma((NC,)),
            dma((NC,)),
            dma((NC, others)),
            dma((NC, others)),
        ],
        compiler_params=pltpu.CompilerParams(
            collective_id=0, has_side_effects=True, vmem_limit_bytes=VMEM_LIMIT
        ),
        cost_estimate=pl.CostEstimate(
            flops=6 * total * width * hid * per_pool,
            bytes_accessed=6 * width * hid * per_pool,
            transcendentals=total * hid * per_pool,
        ),
    )(hidden_in, norm_gain.reshape(1, width), expert_ids, gate_weights, w_gate, w_up, w_down)


VMEM_LIMIT = 63 * 1024 * 1024


def body(hidden_in, norm_gain, expert_ids, gate_weights, w_gate, w_up, w_down):
    batches, rows, width = hidden_in.shape
    per_pool, _, hid = w_gate.shape
    small = lax.axis_size("pool") == 4 and lax.axis_size("sub") == 4
    shaped = batches * rows <= PAD and per_pool == 8 and hid == 384 and width == 4096
    chosen = kernel_body if small and shaped else dense_body
    return chosen(hidden_in, norm_gain, expert_ids, gate_weights, w_gate, w_up, w_down)


def solution(mesh):
    in_specs = (
        P(None, ("group", "pool", "sub"), None),
        P(),
        P(None, ("group", "pool", "sub"), None),
        P(None, ("group", "pool", "sub"), None),
        P("pool", None, "sub"),
        P("pool", None, "sub"),
        P("pool", "sub", None),
    )
    out_specs = P(None, ("group", "pool", "sub"), None)
    return jax.shard_map(body, mesh=mesh, in_specs=in_specs, out_specs=out_specs, check_vma=False)
```

```python
import functools

import jax
import jax.numpy as jnp
from jax import lax
from jax.experimental import pallas as pl
from jax.experimental.pallas import tpu as pltpu
from jax.sharding import PartitionSpec as P


def rms_normed(hidden, norm_gain):
    values = hidden.astype(jnp.float32)
    scale = lax.rsqrt(jnp.mean(values * values, axis=-1, keepdims=True) + 1e-06)
    return (values * scale * norm_gain.astype(jnp.float32)).astype(jnp.bfloat16)


def dense_body(hidden_in, norm_gain, expert_ids, gate_weights, w_gate, w_up, w_down):
    batches, row_count, width = hidden_in.shape
    per_pool, _, hid = w_gate.shape
    pools = lax.axis_size("pool")
    own = batches * row_count
    normed = rms_normed(hidden_in, norm_gain).reshape(own, width)
    experts = jnp.arange(pools * per_pool, dtype=jnp.int32)
    gates = jnp.sum(
        jnp.where(expert_ids[..., None] == experts, gate_weights[..., None].astype(jnp.float32), 0.0), axis=2
    ).astype(jnp.bfloat16).reshape(own, pools * per_pool)
    rows = lax.all_gather(normed, ("pool", "sub"), axis=0, tiled=True)
    gates = lax.all_gather(gates, ("pool", "sub"), axis=0, tiled=True)
    gates = lax.dynamic_slice_in_dim(gates, lax.axis_index("pool") * per_pool, per_pool, axis=1)
    acts = []
    for e in range(per_pool):
        gate_act = jnp.dot(rows, w_gate[e], preferred_element_type=jnp.float32)
        up_act = jnp.dot(rows, w_up[e], preferred_element_type=jnp.float32)
        weight = gates[:, e : e + 1].astype(jnp.float32)
        acts.append((jax.nn.silu(gate_act) * up_act * weight).astype(jnp.bfloat16))
    act = jnp.concatenate(acts, axis=1)
    partial = jnp.dot(act, w_down.reshape(per_pool * hid, width), preferred_element_type=jnp.float32)
    summed = lax.psum_scatter(partial.astype(jnp.bfloat16), ("pool", "sub"), scatter_dimension=0, tiled=True)
    result = hidden_in.reshape(own, width).astype(jnp.float32) + summed.astype(jnp.float32)
    return result.astype(jnp.bfloat16).reshape(batches, row_count, width)


MESH = pl.DeviceIdType.MESH
F32 = jnp.float32
BF16 = jnp.bfloat16
PAD = 16
GW = 128
KC = 4
NC = 8
SLOTS = 12


def expert_kernel(
    subs, hidden, gain, ids, gws, w_gate, w_up, w_down, out,
    xg, xc, acc, act, y, crecv, xsend, xrecv, zsend, zrecv, gu, wd, rowf, sumf, packer_ref, padder_ref,
    gu_sem, wd_sem, az_s, az_r, ax_s, ax_r, ac_s, ac_r,
    rc_s, rc_r, rx_s, rx_r, rz_s, rz_r,
):
    batches, rows, width = hidden.shape
    per_pool, _, hid = w_gate.shape
    kw, nw = width // KC, width // NC
    group, pool, sub = lax.axis_index("group"), lax.axis_index("pool"), lax.axis_index("sub")
    core, side = pool % 2, pool // 2
    block = batches * rows
    quad = subs * PAD
    half = 2 * quad
    cquad = subs * block
    chalf = 2 * cquad
    ctotal = 2 * chalf
    xrow = core * half + side * quad
    own = pl.multiple_of(xrow + sub * PAD, PAD)
    peer_core = (group, side * 2 + 1 - core, sub)
    peer_side = (group, (1 - side) * 2 + core, sub)
    peer_sub = [(group, pool, (sub + d) % subs) for d in range(1, subs)]
    steps = KC * per_pool

    def gu_copies(step):
        slot, e = step % SLOTS, step % per_pool
        krow = pl.multiple_of(step // per_pool * kw, kw)
        return (
            pltpu.make_async_copy(w_gate.at[e, pl.ds(krow, kw), :], gu.at[slot, :, pl.ds(0, hid)], gu_sem.at[slot, 0]),
            pltpu.make_async_copy(w_up.at[e, pl.ds(krow, kw), :], gu.at[slot, :, pl.ds(hid, hid)], gu_sem.at[slot, 1]),
        )

    def wd_copy(n):
        return pltpu.make_async_copy(
            w_down.at[:, :, pl.ds(pl.multiple_of(n * nw, nw), nw)], wd.at[n], wd_sem.at[n]
        )

    def first(step, carry):
        for copy in gu_copies(step):
            copy.start()
        return carry

    lax.fori_loop(0, SLOTS, first, 0)

    barrier = pltpu.get_barrier_semaphore()
    for peer in [peer_core, peer_side] + peer_sub:
        pl.semaphore_signal(barrier, inc=1, device_id=peer, device_id_type=MESH)

    rowf[...] = jnp.zeros_like(rowf)
    lane = lax.broadcasted_iota(jnp.int32, (rows, GW), 1)
    gain_row = gain[...].astype(F32)
    for m in range(batches):
        values = hidden[m].astype(F32)
        scale = lax.rsqrt(jnp.mean(values * values, axis=-1, keepdims=True) + 1e-06)
        rowf[rows * m : rows * (m + 1), GW:] = values * scale * gain_row
        names, weights = ids[m], gws[m].astype(F32)
        table = jnp.zeros((rows, GW), F32)
        for k in range(names.shape[1]):
            table = table + jnp.where(names[:, k : k + 1] == lane, weights[:, k : k + 1], 0.0)
        rowf[rows * m : rows * (m + 1), :GW] = table
    xg[pl.ds(own, PAD), :] = rowf[...].astype(BF16)

    pl.semaphore_wait(barrier, subs + 1)

    def cols(c):
        return pl.ds(0, GW + kw) if c == 0 else pl.ds(GW + c * kw, kw)

    def az(c, d):
        ref = xg.at[pl.ds(own, PAD), cols(c)]
        return pltpu.make_async_remote_copy(
            ref, ref, az_s.at[c, d], az_r.at[c, d], device_id=peer_sub[d], device_id_type=MESH
        )

    def az_wait(c):
        for d in range(subs - 1):
            az(c, d).wait_recv()

    def ax(c):
        ref = xg.at[pl.ds(pl.multiple_of(xrow, PAD), quad), cols(c)]
        return pltpu.make_async_remote_copy(
            ref, ref, ax_s.at[c], ax_r.at[c], device_id=peer_side, device_id_type=MESH
        )

    def ac(c):
        ref = xg.at[pl.ds(pl.multiple_of(core * half, PAD), half), cols(c)]
        return pltpu.make_async_remote_copy(
            ref, ref, ac_s.at[c], ac_r.at[c], device_id=peer_core, device_id_type=MESH
        )

    def relay_x(c):
        az_wait(c)
        ax(c).start()

    def relay_c(c):
        ax(c).wait_recv()
        ac(c).start()

    for c in range(KC):
        for d in range(subs - 1):
            az(c, d).start()
    acc[...] = jnp.zeros_like(acc)
    relay_x(0)
    relay_x(1)
    relay_c(0)
    relay_x(2)

    source = lax.broadcasted_iota(jnp.int32, (ctotal, 2 * half), 1)
    target = lax.broadcasted_iota(jnp.int32, (ctotal, 2 * half), 0)
    inside = source & (PAD - 1)
    packer = ((target == (source >> 4) * block + inside) & (inside < block)).astype(F32).astype(BF16)
    source = lax.broadcasted_iota(jnp.int32, (quad, cquad), 1)
    target = lax.broadcasted_iota(jnp.int32, (quad, cquad), 0)
    inside = target & (PAD - 1)
    padder_ref[...] = (
        ((source == (target >> 4) * block + inside) & (inside < block)).astype(F32).astype(BF16)
    )
    packer_ref[...] = packer

    def gu_step(c, step, carry):
        slot, e = step % SLOTS, step % per_pool
        for copy in gu_copies(step):
            copy.wait()
        total = acc[e] + jnp.dot(
            xc[:, GW + c * kw : GW + (c + 1) * kw], gu[slot], preferred_element_type=F32
        )
        if c < KC - 1:
            acc[e] = total
        else:
            g, u = total[:, :hid], total[:, hid:]
            lanes = lax.broadcasted_iota(jnp.int32, (ctotal, GW), 1)
            weight = jnp.sum(
                jnp.where(lanes == pool * per_pool + e, xc[:, :GW].astype(F32), 0.0), axis=1, keepdims=True
            )
            act[:, pl.ds(pl.multiple_of(e * hid, hid), hid)] = (
                g / (1.0 + jnp.exp(-g)) * u * weight
            ).astype(BF16)

        @pl.when(step + SLOTS < steps)
        def _():
            for copy in gu_copies(step + SLOTS):
                copy.start()

        extra = step + SLOTS - steps

        @pl.when((extra >= 0) & (extra < NC))
        def _():
            wd_copy(extra).start()

        return carry

    cut = per_pool // 2
    for c in range(KC):
        ac(c).wait_recv()
        low = 0 if c == 0 else GW + c * kw
        high = GW + (c + 1) * kw
        xc[:, low:high] = jnp.dot(
            packer_ref[...], xg[:, low:high], preferred_element_type=F32
        ).astype(BF16)
        base = c * per_pool
        lax.fori_loop(base, base + cut, functools.partial(gu_step, c), 0)
        if c + 3 < KC:
            relay_x(c + 3)
        if c + 1 < KC:
            relay_c(c + 1)
        lax.fori_loop(base + cut, base + per_pool, functools.partial(gu_step, c), 0)

    def ncols(n):
        return pl.ds(pl.multiple_of(n * nw, nw), nw)

    def rc(n):
        return pltpu.make_async_remote_copy(
            y.at[pl.ds(pl.multiple_of((1 - core) * chalf, PAD), chalf), ncols(n)], crecv.at[:, ncols(n)],
            rc_s.at[n], rc_r.at[n], device_id=peer_core, device_id_type=MESH,
        )

    def rx(n):
        return pltpu.make_async_remote_copy(
            xsend.at[:, ncols(n)], xrecv.at[:, ncols(n)],
            rx_s.at[n], rx_r.at[n], device_id=peer_side, device_id_type=MESH,
        )

    def rz(n, d):
        row = pl.multiple_of((sub + d + 1) % subs * PAD, PAD)
        return pltpu.make_async_remote_copy(
            zsend.at[pl.ds(row, PAD), ncols(n)], zrecv.at[d, :, ncols(n)],
            rz_s.at[n, d], rz_r.at[n, d], device_id=peer_sub[d], device_id_type=MESH,
        )

    def down_step(n, carry):
        @pl.when(n < NC)
        def _():
            wd_copy(n).wait()
            y[:, ncols(n)] = jnp.dot(
                act[...], wd[n].reshape(per_pool * hid, nw), preferred_element_type=F32
            ).astype(BF16)
            rc(n).start()

        @pl.when((n >= 1) & (n < NC + 1))
        def _():
            m = n - 1
            rc(m).wait_recv()
            far = pl.multiple_of((1 - side) * cquad, PAD)
            xsend[:, ncols(m)] = (
                y[pl.ds(pl.multiple_of(core * chalf + (1 - side) * cquad, PAD), cquad), ncols(m)].astype(F32)
                + crecv[pl.ds(far, cquad), ncols(m)].astype(F32)
            ).astype(BF16)
            rx(m).start()

        @pl.when((n >= 3) & (n < NC + 3))
        def _():
            m = n - 3
            rx(m).wait_recv()
            near = pl.multiple_of(side * cquad, PAD)
            chosen = (
                y[pl.ds(pl.multiple_of(core * chalf + side * cquad, PAD), cquad), ncols(m)].astype(F32)
                + crecv[pl.ds(near, cquad), ncols(m)].astype(F32)
                + xrecv[:, ncols(m)].astype(F32)
            ).astype(BF16)
            zsend[:, ncols(m)] = jnp.dot(
                padder_ref[...], chosen, preferred_element_type=F32
            ).astype(BF16)
            for d in range(subs - 1):
                rz(m, d).start()

        @pl.when(n >= 5)
        def _():
            m = n - 5
            total = zsend[pl.ds(pl.multiple_of(sub * PAD, PAD), PAD), ncols(m)].astype(F32)
            for d in range(subs - 1):
                rz(m, d).wait_recv()
                total = total + zrecv[d, :, ncols(m)].astype(F32)
            sumf[...] = total
            for b in range(batches):
                out[b, :, ncols(m)] = (
                    hidden[b, :, ncols(m)].astype(F32) + sumf[rows * b : rows * (b + 1), :]
                ).astype(BF16)

        return carry

    lax.fori_loop(0, NC + 5, down_step, 0)

    for c in range(KC):
        for d in range(subs - 1):
            az(c, d).wait_send()
        ax(c).wait_send()
        ac(c).wait_send()

    def sent(n, carry):
        rc(n).wait_send()
        rx(n).wait_send()
        for d in range(subs - 1):
            rz(n, d).wait_send()
        return carry

    lax.fori_loop(0, NC, sent, 0)


def kernel_body(hidden_in, norm_gain, expert_ids, gate_weights, w_gate, w_up, w_down):
    batches, rows, width = hidden_in.shape
    per_pool, _, hid = w_gate.shape
    subs = lax.axis_size("sub")
    total = 4 * subs * PAD
    ctotal = 4 * subs * batches * rows
    vmem = pl.BlockSpec(memory_space=pltpu.VMEM)
    hbm = pl.BlockSpec(memory_space=pl.ANY)
    dma = pltpu.SemaphoreType.DMA
    others = subs - 1
    return pl.pallas_call(
        functools.partial(expert_kernel, subs),
        out_shape=jax.ShapeDtypeStruct(hidden_in.shape, BF16),
        in_specs=[vmem] * 4 + [hbm] * 3,
        out_specs=vmem,
        scratch_shapes=[
            pltpu.VMEM((total, GW + width), BF16),
            pltpu.VMEM((ctotal, GW + width), BF16),
            pltpu.VMEM((per_pool, ctotal, 2 * hid), F32),
            pltpu.VMEM((ctotal, per_pool * hid), BF16),
            pltpu.VMEM((ctotal, width), BF16),
            pltpu.VMEM((ctotal // 2, width), BF16),
            pltpu.VMEM((ctotal // 4, width), BF16),
            pltpu.VMEM((ctotal // 4, width), BF16),
            pltpu.VMEM((total // 4, width), BF16),
            pltpu.VMEM((others, PAD, width), BF16),
            pltpu.VMEM((SLOTS, width // KC, 2 * hid), BF16),
            pltpu.VMEM((NC, per_pool, hid, width // NC), BF16),
            pltpu.VMEM((PAD, GW + width), F32),
            pltpu.VMEM((PAD, width // NC), F32),
            pltpu.VMEM((ctotal, total), BF16),
            pltpu.VMEM((total // 4, ctotal // 4), BF16),
            dma((SLOTS, 2)),
            dma((NC,)),
            dma((KC, others)),
            dma((KC, others)),
            dma((KC,)),
            dma((KC,)),
            dma((KC,)),
            dma((KC,)),
            dma((NC,)),
            dma((NC,)),
            dma((NC,)),
            dma((NC,)),
            dma((NC, others)),
            dma((NC, others)),
        ],
        compiler_params=pltpu.CompilerParams(
            collective_id=0, has_side_effects=True, vmem_limit_bytes=VMEM_LIMIT
        ),
        cost_estimate=pl.CostEstimate(
            flops=6 * total * width * hid * per_pool,
            bytes_accessed=6 * width * hid * per_pool,
            transcendentals=total * hid * per_pool,
        ),
    )(hidden_in, norm_gain.reshape(1, width), expert_ids, gate_weights, w_gate, w_up, w_down)


VMEM_LIMIT = 63 * 1024 * 1024


def body(hidden_in, norm_gain, expert_ids, gate_weights, w_gate, w_up, w_down):
    batches, rows, width = hidden_in.shape
    per_pool, _, hid = w_gate.shape
    small = lax.axis_size("pool") == 4 and lax.axis_size("sub") == 4
    shaped = batches * rows == 12 and per_pool == 8 and hid == 384 and width == 4096
    chosen = kernel_body if small and shaped else dense_body
    return chosen(hidden_in, norm_gain, expert_ids, gate_weights, w_gate, w_up, w_down)


def solution(mesh):
    in_specs = (
        P(None, ("group", "pool", "sub"), None),
        P(),
        P(None, ("group", "pool", "sub"), None),
        P(None, ("group", "pool", "sub"), None),
        P("pool", None, "sub"),
        P("pool", None, "sub"),
        P("pool", "sub", None),
    )
    out_specs = P(None, ("group", "pool", "sub"), None)
    return jax.shard_map(body, mesh=mesh, in_specs=in_specs, out_specs=out_specs, check_vma=False)
```
